128 devices in a mesh: vid: 8 (over x, core), fsdp: 16 (over y, z).
Axes of the slice: x: 4, y: 4, z: 4, core: 2. Of those that a mesh axis runs over, the one named last changes fastest.
Arguments:
- latents: bfloat16 [64, 256, 6144], P('vid', 'fsdp'), may hold values from -6 to 6
- shift_mod: float32 [64, 6144], P('vid'), may hold values from -3 to 3
- scale_mod: float32 [64, 6144], P('vid'), may hold values from -3 to 3
- qkv_weight: bfloat16 [6144, 3, 4096], P(None, None, 'fsdp'), may hold values from -0.078125 to 0.078125
- kv_cache: bfloat16 [64, 4, 2, 256, 4096], P('vid', None, None, None, 'fsdp'), may hold values from -6 to 6
- holders: int32 [64], replicated, may hold values from 0 to 63, as said below
- cached: int32 [64], replicated, may hold values from 1 to 4
Outputs:
- attended: bfloat16 [64, 256, 4096], P('vid', None, 'fsdp')
The draws below stay inside these ranges and needn't reach their ends.
Inputs may be any that keep to these rules, and one draw needn't show every extreme that they name: holders is a permutation of the 64 cache slots. Slot s lies on index s // 8 of vid; the owner of video v is index v // 8 of vid. Each index of vid holds exactly one video of each owner.
All inputs are finite; a program needn't handle non-finite values.
Results may differ from the reference program's by a relative error of at most 0.0048.
Values may be sent and summed in bfloat16 or wider, within the bound.
No kernel may reach another device: no remote copies, remote signals or barrier semaphores. Data moves between devices by JAX's collectives and lax.ppermute only.
A program may use at most 192 MiB of HBM per device.

```python
import math
import jax
import jax.numpy as jnp
from jax import lax

D = 6144
HEADS = 32
HEAD = 128
VID_DEV = 8
GROUP_TOKENS = 256
MAXC = 4
VIDEOS = 64
N_VID = 8


def draw_holders(key, part):
    key = jax.random.fold_in(key, 11)
    owner_keys = jax.random.split(jax.random.fold_in(key, 1), N_VID)
    offsets = jax.vmap(lambda single: jax.random.permutation(single, VID_DEV))(owner_keys).astype(jnp.int32)
    owners = jnp.arange(VIDEOS, dtype=jnp.int32) // VID_DEV
    local_index = jnp.arange(VIDEOS, dtype=jnp.int32) % VID_DEV
    shifted = offsets[owners, local_index]
    holder = (owners + shifted) % N_VID
    within = shifted // N_VID * N_VID + owners
    holder_keys = jax.random.split(jax.random.fold_in(key, 2), N_VID)
    scramble = jax.vmap(lambda single: jax.random.permutation(single, VID_DEV))(holder_keys).astype(jnp.int32)
    return (holder * VID_DEV + scramble[holder, within]).astype(jnp.int32)


def draw_cached(key, part):
    key = jax.random.fold_in(key, 23)
    counts = jax.random.randint(jax.random.fold_in(key, 1), (VIDEOS,), 1, MAXC + 1, dtype=jnp.int32)
    longest = jax.random.randint(jax.random.fold_in(key, 2), (), 0, VIDEOS, dtype=jnp.int32)
    shortest = (longest + 1 + jax.random.randint(jax.random.fold_in(key, 3), (), 0, VIDEOS - 1, dtype=jnp.int32)) % VIDEOS
    return counts.at[longest].set(MAXC).at[shortest].set(1).astype(jnp.int32)


def level_of(stream_key, extent, pieces, least, largest):
    gain = 1.0
    for dim, parts in pieces:
        heights = jax.random.uniform(jax.random.fold_in(jax.random.fold_in(stream_key, 6), dim), (parts,), jnp.float32, least / len(pieces), largest / len(pieces))
        gain = gain * jnp.repeat(jnp.exp(heights), extent[dim] // parts).reshape((-1,) + (1,) * (len(extent) - 1 - dim))
    return gain


def noise(own_key, shape, scale, bound, cuts=(), kind=jnp.bfloat16):
    array = scale * jax.random.normal(own_key, shape, jnp.float32)
    if cuts:
        array = array * level_of(own_key, shape, cuts, -0.22, 0.18)
    return jnp.clip(array, -bound, bound).astype(kind)


def setup_inputs(seed: int = 0) -> dict:
    key_of = jax.random.split(jax.random.key(seed), 8)
    latents = noise(key_of[0], (VIDEOS, GROUP_TOKENS, D), 1.0, 6.0, ((0, 8), (1, 16)))
    shift_mod = noise(key_of[1], (VIDEOS, D), 0.5, 3.0, ((0, 8),), jnp.float32)
    scale_mod = noise(key_of[2], (VIDEOS, D), 0.5, 3.0, ((0, 8),), jnp.float32)
    qkv_weight = noise(key_of[3], (D, 3, HEADS * HEAD), D ** -0.5, 0.078125, ((2, 16),))
    kv_cache = noise(key_of[4], (VIDEOS, MAXC, 2, GROUP_TOKENS, HEADS * HEAD), 1.0, 6.0, ((0, 8), (4, 16)))
    holders = draw_holders(jax.random.fold_in(key_of[7], 71), 0)
    cached = draw_cached(jax.random.fold_in(key_of[7], 71), 0)
    return dict(latents=latents, shift_mod=shift_mod, scale_mod=scale_mod, qkv_weight=qkv_weight, kv_cache=kv_cache, holders=holders, cached=cached)


def rms_scale(values):
    return values * lax.rsqrt(lax.optimization_barrier(jnp.mean(values * values, axis=-1, keepdims=True)) + 1e-06)

def modulate(latent_rows, shift_row, scale_row):
    widened = latent_rows.astype(jnp.float32)
    center = lax.optimization_barrier(jnp.mean(widened, axis=-1, keepdims=True))
    offsets = widened - center
    spread = lax.optimization_barrier(jnp.mean(offsets * offsets, axis=-1, keepdims=True))
    return (offsets * lax.rsqrt(spread + 1e-06) * (1.0 + scale_row) + shift_row).astype(jnp.bfloat16)

def reference(latents, shift_mod, scale_mod, qkv_weight, kv_cache, holders, cached):
    weight_matrix = qkv_weight.reshape(D, 3 * HEADS * HEAD)

    def one_video(inputs):
        latent_rows, shift_row, scale_row, holder_slot, active_count = inputs
        normed = modulate(latent_rows, shift_row[None, :], scale_row[None, :])
        projected = jnp.dot(normed, weight_matrix, preferred_element_type=jnp.float32).reshape(GROUP_TOKENS, 3, HEADS, HEAD)
        query_rows = lax.optimization_barrier(rms_scale(projected[:, 0]).astype(jnp.bfloat16))
        current_keys = rms_scale(projected[:, 1]).astype(jnp.bfloat16)
        current_values = projected[:, 2].astype(jnp.bfloat16)
        slot_blocks = lax.dynamic_index_in_dim(kv_cache, holder_slot.astype(jnp.int32), 0, keepdims=False)
        previous_keys = rms_scale(slot_blocks[:, 0].astype(jnp.float32).reshape(MAXC * GROUP_TOKENS, HEADS, HEAD)).astype(jnp.bfloat16)
        previous_values = slot_blocks[:, 1].reshape(MAXC * GROUP_TOKENS, HEADS, HEAD)
        all_keys = lax.optimization_barrier(jnp.concatenate([current_keys, previous_keys], axis=0))
        all_values = lax.optimization_barrier(jnp.concatenate([current_values, previous_values], axis=0))
        token_positions = jnp.arange(MAXC * GROUP_TOKENS, dtype=jnp.int32) // GROUP_TOKENS
        active_flags = jnp.concatenate([jnp.ones((GROUP_TOKENS,), jnp.float32), (token_positions < active_count).astype(jnp.float32)])
        logit_scores = jnp.einsum('qhd,khd->hqk', query_rows.astype(jnp.float32), all_keys.astype(jnp.float32)) / math.sqrt(HEAD)
        softmax_weights = jnp.exp(logit_scores) * active_flags[None, None, :]
        totals = lax.optimization_barrier(jnp.sum(softmax_weights, axis=-1))
        rounded_weights = lax.optimization_barrier(softmax_weights.astype(jnp.bfloat16))
        summed = jnp.einsum('hqk,khd->qhd', rounded_weights.astype(jnp.float32), all_values.astype(jnp.float32))
        return (summed / jnp.transpose(totals)[:, :, None]).astype(jnp.bfloat16).reshape(GROUP_TOKENS, HEADS * HEAD)
    return lax.map(one_video, (latents, shift_mod, scale_mod, holders, cached))
```

```python
import math

import jax
import jax.numpy as jnp
from jax import lax
from jax.experimental import pallas as pl
from jax.experimental.pallas import tpu as pltpu
from jax.sharding import PartitionSpec as P

HEAD = 128
GROUP = 256
MAXC = 4
D = 6144
ROWS = 16
KB = 1024
SCALE = 1.0 / math.sqrt(HEAD)
VMEM = 56 * 1024 * 1024


def rms_scale(values):
    return values * lax.rsqrt(jnp.mean(values * values, axis=-1, keepdims=True) + 1e-06)


def norm_body(first, lat_ref, shift_ref, scale_ref, out_ref):
    v = pl.program_id(0) + first
    x = lat_ref[0].astype(jnp.float32)
    center = jnp.mean(x, axis=-1, keepdims=True)
    offsets = x - center
    spread = jnp.mean(offsets * offsets, axis=-1, keepdims=True)
    gain = 1.0 + scale_ref[pl.ds(v, 1), :]
    out = offsets * lax.rsqrt(spread + 1e-06) * gain + shift_ref[pl.ds(v, 1), :]
    out_ref[0] = out.astype(jnp.bfloat16)


def norm(latents, shift, scale, first, count):
    whole = pl.BlockSpec(shift.shape, lambda i: (0, 0))
    return pl.pallas_call(
        lambda *refs: norm_body(first, *refs),
        grid=(count,),
        in_specs=[
            pl.BlockSpec((1,) + latents.shape[1:], lambda i: (i + first, 0, 0)),
            whole,
            whole,
        ],
        out_specs=pl.BlockSpec((1,) + latents.shape[1:], lambda i: (i, 0, 0)),
        out_shape=jax.ShapeDtypeStruct((count,) + latents.shape[1:], jnp.bfloat16),
        compiler_params=pltpu.CompilerParams(vmem_limit_bytes=VMEM),
        name="norm",
    )(latents, shift, scale)


def reorder(cache, order):
    block = (1,) + cache.shape[1:]
    return pl.pallas_call(
        lambda order_ref, src, dst: dst.__setitem__(..., src[...]),
        grid_spec=pltpu.PrefetchScalarGridSpec(
            num_scalar_prefetch=1,
            grid=(cache.shape[0],),
            in_specs=[pl.BlockSpec(block, lambda i, o: (o[i], 0, 0, 0, 0))],
            out_specs=pl.BlockSpec(block, lambda i, o: (i, 0, 0, 0, 0)),
        ),
        out_shape=jax.ShapeDtypeStruct(cache.shape, cache.dtype),
        compiler_params=pltpu.CompilerParams(vmem_limit_bytes=VMEM),
        name="reorder",
    )(order, cache)


def add_keys(q, keys, values, acc_ref, first):
    logits = lax.dot_general(
        q, keys, (((1,), (1,)), ((), ())), preferred_element_type=jnp.float32
    )
    weights = jnp.exp(logits * SCALE).astype(jnp.bfloat16)
    wide = jnp.concatenate([values, jnp.ones_like(values)], axis=1)
    part = jnp.dot(weights, wide, preferred_element_type=jnp.float32)
    if first:
        acc_ref[...] = part
    else:
        acc_ref[...] += part


def attend_body(chunk, place_ref, count_ref, pos_ref, *refs):
    tokens, (w_ref, kv_a, kv_b, out_ref, acc_ref, sum_ref) = refs[:8], refs[8:]
    k = pl.program_id(0)

    @pl.when(k == 0)
    def _():
        acc_ref[...] = jnp.zeros_like(acc_ref)

    x = jnp.concatenate([t[...] for t in tokens], axis=0)
    for j in range(3):
        acc_ref[j] += jnp.dot(x, w_ref[j], preferred_element_type=jnp.float32)

    @pl.when(k == pl.num_programs(0) - 1)
    def _():
        y, z, sign = pos_ref[0], pos_ref[1], pos_ref[2]
        for i, kv in ((0, kv_a), (1, kv_b)):
            rows = pl.ds(i * GROUP, GROUP)
            live = count_ref[chunk + 4 * i]
            queries = []
            for h in range(2):
                lanes = pl.ds(h * HEAD, HEAD)
                q = rms_scale(acc_ref[0, rows, lanes]).astype(jnp.bfloat16)
                key = rms_scale(acc_ref[1, rows, lanes]).astype(jnp.bfloat16)
                add_keys(q, key, acc_ref[2, rows, lanes].astype(jnp.bfloat16), sum_ref.at[h], True)
                queries.append(q)
            for g in range(MAXC):

                @pl.when(g < live)
                def _():
                    for h in range(2):
                        lanes = pl.ds(h * HEAD, HEAD)
                        old = rms_scale(kv[0, g, 0, :, lanes].astype(jnp.float32))
                        add_keys(
                            queries[h],
                            old.astype(jnp.bfloat16),
                            kv[0, g, 1, :, lanes],
                            sum_ref.at[h],
                            False,
                        )

            out = jnp.concatenate(
                [sum_ref[h, :, :HEAD] / sum_ref[h, :, HEAD:] for h in range(2)], axis=1
            ).astype(jnp.bfloat16)
            for outer in range(4):
                for inner in range(4):
                    a = (y - sign * (inner if i == 0 else outer)) & 3
                    b = (z - sign * (outer if i == 0 else inner)) & 3
                    start = pl.multiple_of((a * 4 + b) * ROWS, ROWS)
                    at = (outer * 4 + inner) * ROWS
                    out_ref[i, pl.ds(start, ROWS), :] = out[at : at + ROWS]


def attend(chunk, tokens, weights, cache, places, counts, pos):
    kv_block = (1,) + cache.shape[1:]
    token_spec = pl.BlockSpec((4 * ROWS, KB), lambda k, *s: (0, k))
    return pl.pallas_call(
        lambda *refs: attend_body(chunk, *refs),
        grid_spec=pltpu.PrefetchScalarGridSpec(
            num_scalar_prefetch=3,
            grid=(D // KB,),
            in_specs=[token_spec] * 8
            + [
                pl.BlockSpec((3, KB, 2 * HEAD), lambda k, *s: (0, k, 0)),
                pl.BlockSpec(kv_block, lambda k, p, c, q: (p[chunk], 0, 0, 0, 0)),
                pl.BlockSpec(kv_block, lambda k, p, c, q: (p[chunk + 4], 0, 0, 0, 0)),
            ],
            out_specs=pl.BlockSpec((2, GROUP, 2 * HEAD), lambda k, *s: (0, 0, 0)),
            scratch_shapes=[
                pltpu.VMEM((3, 2 * GROUP, 2 * HEAD), jnp.float32),
                pltpu.VMEM((2, GROUP, 2 * HEAD), jnp.float32),
            ],
        ),
        out_shape=jax.ShapeDtypeStruct((2, GROUP, 2 * HEAD), jnp.bfloat16),
        compiler_params=pltpu.CompilerParams(vmem_limit_bytes=VMEM),
        cost_estimate=pl.CostEstimate(
            flops=2 * 512 * D * 768, bytes_accessed=18 << 20, transcendentals=1 << 20
        ),
        name="attend",
    )(places, counts, pos, *tokens, weights, cache, cache)


def ring(dy, dz):
    pairs = []
    for vid in range(8):
        s = 1 if vid % 2 == 0 else -1
        for y in range(4):
            for z in range(4):
                to = (y + s * dy) % 4 * 4 + (z + s * dz) % 4
                pairs.append((vid * 16 + y * 4 + z, vid * 16 + to))
    return pairs


def send(value, pairs):
    return lax.ppermute(value, ("vid", "fsdp"), pairs)


def shards(latents, shift_mod, scale_mod, qkv_weight, kv_cache, holders, cached):
    vid = lax.axis_index("vid")
    fsdp = lax.axis_index("fsdp")
    along_y, along_z = ring(1, 0), ring(0, 1)
    weights = jnp.transpose(qkv_weight, (1, 0, 2))

    ya = [norm(latents, shift_mod, scale_mod, 0, 4)]
    zb = [norm(latents, shift_mod, scale_mod, 4, 4)]
    for _ in range(3):
        ya.append(send(ya[-1], along_y))
        zb.append(send(zb[-1], along_z))

    by_owner = holders.reshape(8, 8)
    order = jnp.sum(jnp.where(by_owner // 8 == vid, by_owner % 8, 0), axis=1, dtype=jnp.int32)
    places = lax.dynamic_slice_in_dim(holders, vid * 8, 8) // 8
    counts = lax.dynamic_slice_in_dim(cached, vid * 8, 8)
    pos = jnp.stack([fsdp // 4, fsdp % 4, 1 - 2 * (vid % 2)]).astype(jnp.int32)
    cache = lax.all_to_all(
        reorder(kv_cache, order), "vid", split_axis=0, concat_axis=0, tiled=True
    )

    outs = []
    for c in range(4):
        a = [jnp.concatenate([block[c] for block in ya], axis=0)]
        b = [jnp.concatenate([block[c] for block in zb], axis=0)]
        for _ in range(3):
            a.append(send(a[-1], along_z))
            b.append(send(b[-1], along_y))
        outs.append(attend(c, a + b, weights, cache, places, counts, pos))
    return jnp.concatenate([o[:1] for o in outs] + [o[1:] for o in outs], axis=0)


def solution(mesh):
    return jax.shard_map(
        shards,
        mesh=mesh,
        in_specs=(
            P("vid", "fsdp", None),
            P("vid", None),
            P("vid", None),
            P(None, None, "fsdp"),
            P("vid", None, None, None, "fsdp"),
            P(),
            P(),
        ),
        out_specs=P("vid", None, "fsdp"),
        check_vma=False,
    )
```

```python
import math

import jax
import jax.numpy as jnp
from jax import lax
from jax.experimental import pallas as pl
from jax.experimental.pallas import tpu as pltpu
from jax.sharding import PartitionSpec as P

HEAD = 128
GROUP = 256
MAXC = 4
D = 6144
ROWS = 16
WIDTH = 2 * HEAD
SCALE = 1.0 / math.sqrt(HEAD)
HBM = pl.BlockSpec(memory_space=pltpu.HBM)
VMEM = pl.BlockSpec(memory_space=pltpu.VMEM)
SMEM = pl.BlockSpec(memory_space=pltpu.SMEM)
MIB = 1024 * 1024

def rms_scale(values):
    return values * lax.rsqrt(jnp.mean(values * values, axis=-1, keepdims=True) + 1e-06)


def norm_body(count, lat_ref, shift_ref, scale_ref, *refs):
    *outs, in_ref, add_ref, gain_ref, sem = refs
    per = count // len(outs)
    planes = [
        pltpu.make_async_copy(shift_ref, add_ref, sem.at[count]),
        pltpu.make_async_copy(scale_ref, gain_ref, sem.at[count + 1]),
    ]
    rows = [
        pltpu.make_async_copy(lat_ref.at[i], in_ref.at[i], sem.at[i]) for i in range(count)
    ]
    for copy in planes + rows:
        copy.start()
    for copy in planes:
        copy.wait()
    for i in range(count):
        rows[i].wait()
        x = in_ref[i].astype(jnp.float32)
        offsets = x - jnp.mean(x, axis=-1, keepdims=True)
        spread = jnp.mean(offsets * offsets, axis=-1, keepdims=True)
        out = offsets * lax.rsqrt(spread + 1e-06) * (1.0 + gain_ref[i : i + 1]) + add_ref[i : i + 1]
        at = i % per * ROWS
        outs[i // per][at : at + ROWS] = out.astype(jnp.bfloat16)


def norm(latents, shift, scale, parts):
    count = latents.shape[0]
    rows = jax.ShapeDtypeStruct((count // parts * ROWS, D), jnp.bfloat16)
    return pl.pallas_call(
        lambda *refs: norm_body(count, *refs),
        in_specs=[HBM] * 3,
        out_specs=[VMEM] * parts,
        scratch_shapes=[
            pltpu.VMEM((count, ROWS, D), jnp.bfloat16),
            pltpu.VMEM((count, D), jnp.float32),
            pltpu.VMEM((count, D), jnp.float32),
            pltpu.SemaphoreType.DMA((count + 2,)),
        ],
        out_shape=[rows] * parts,
        compiler_params=pltpu.CompilerParams(vmem_limit_bytes=56 * MIB),
        name="norm",
    )(latents, shift, scale)


def reorder_body(count, holders_ref, cached_ref, cache_ref, *refs):
    out_ref, plan_ref, held_ref, sem = refs[-4:]
    vid, fsdp = lax.axis_index("vid"), lax.axis_index("fsdp")

    def load(i):
        slot = jnp.int32(0)
        for v in range(count):
            holder = holders_ref[i * count + v]
            slot = jnp.where((holder >> 3) == vid, holder & 7, slot)
        return pltpu.make_async_copy(cache_ref.at[slot], held_ref.at[i], sem.at[0, i])

    def store(i):
        return pltpu.make_async_copy(held_ref.at[i], out_ref.at[i], sem.at[1, i])

    loads = [load(i) for i in range(count)]
    for copy in loads[:3]:
        copy.start()
    for v in range(count):
        plan_ref[v] = holders_ref[vid * count + v] >> 3
        plan_ref[8 + v] = cached_ref[vid * count + v]
    plan_ref[24] = fsdp >> 2
    plan_ref[25] = fsdp & 3
    plan_ref[26] = 1 - 2 * (vid & 1)
    for i in range(count):
        loads[i].wait()
        store(i).start()
        if i + 3 < count:
            loads[i + 3].start()
    for i in range(count):
        store(i).wait()


def reorder(holders, cached, cache, *earlier):
    count = cache.shape[0]
    return pl.pallas_call(
        lambda *refs: reorder_body(count, *refs),
        in_specs=[SMEM] * 2 + [HBM] * (1 + len(earlier)),
        out_specs=[HBM, SMEM],
        scratch_shapes=[
            pltpu.VMEM(cache.shape, cache.dtype),
            pltpu.SemaphoreType.DMA((2, count)),
        ],
        out_shape=[
            jax.ShapeDtypeStruct(cache.shape, cache.dtype),
            jax.ShapeDtypeStruct((32,), jnp.int32),
        ],
        compiler_params=pltpu.CompilerParams(vmem_limit_bytes=56 * MIB),
        name="reorder",
    )(holders, cached, cache, *earlier)


def project_body(count, *refs):
    tokens, w_ref, out_ref = refs[:count], refs[count], refs[count + 1]
    x_ref, sem = refs[count + 2 :]
    parts = sem.shape[1]
    depth = D // parts

    def fetch(i, k):
        rows = tokens[i].shape[0]
        return pltpu.make_async_copy(
            tokens[i].at[:, pl.ds(k * depth, depth)],
            x_ref.at[pl.ds(i * rows, rows), pl.ds(k * depth, depth)],
            sem.at[i, k],
        )

    for k in range(parts):
        for i in range(count):
            fetch(i, k).start()
    totals = [None] * 3
    for k in range(parts):
        for i in range(count):
            fetch(i, k).wait()
        x = x_ref[:, pl.ds(k * depth, depth)]
        for j in range(3):
            part = jnp.dot(x, w_ref[j, pl.ds(k * depth, depth)], preferred_element_type=jnp.float32)
            totals[j] = part if totals[j] is None else totals[j] + part
    for j in range(3):
        for h in range(2):
            rows = totals[j][:, h * HEAD : (h + 1) * HEAD]
            if j < 2:
                rows = rms_scale(rows)
            out_ref[j, :, h * HEAD : (h + 1) * HEAD] = rows.astype(jnp.bfloat16)


def project(tokens, weights):
    count = len(tokens)
    rows = count * tokens[0].shape[0]
    return pl.pallas_call(
        lambda *refs: project_body(count, *refs),
        in_specs=[HBM] * count + [VMEM],
        out_specs=VMEM,
        scratch_shapes=[
            pltpu.VMEM((rows, D), jnp.bfloat16),
            pltpu.SemaphoreType.DMA((count, 3)),
        ],
        out_shape=jax.ShapeDtypeStruct((3, rows, WIDTH), jnp.bfloat16),
        compiler_params=pltpu.CompilerParams(vmem_limit_bytes=32 * MIB),
        cost_estimate=pl.CostEstimate(
            flops=2 * rows * D * 768, bytes_accessed=rows * D * 2, transcendentals=0
        ),
        name="project",
    )(*tokens, weights)


def add_keys(q, keys, values, acc_ref, first):
    logits = lax.dot_general(
        q, keys, (((1,), (1,)), ((), ())), preferred_element_type=jnp.float32
    )
    weights = jnp.exp(logits * SCALE).astype(jnp.bfloat16)
    wide = jnp.concatenate([values, jnp.ones_like(values)], axis=1)
    part = jnp.dot(weights, wide, preferred_element_type=jnp.float32)
    if first:
        acc_ref[...] = part
    else:
        acc_ref[...] += part


def attend_body(videos, plan_ref, *refs):
    n = len(videos)
    steps, cache_ref = refs[:4], refs[4]
    out_ref, old_ref, sum_ref, rows_ref, in_sem, out_sem = refs[-6:]
    y, z, sign = plan_ref[24], plan_ref[25], plan_ref[26]

    def fetch(i, g):
        place = plan_ref[videos[i]]
        return pltpu.make_async_copy(cache_ref.at[place, g], old_ref.at[i, g], in_sem.at[i, g])

    def store(i):
        return pltpu.make_async_copy(rows_ref.at[i], out_ref.at[videos[i]], out_sem.at[i])

    for i in range(n):
        for g in range(MAXC):

            @pl.when(g < plan_ref[8 + videos[i]])
            def _():
                fetch(i, g).start()

    for i in range(n):
        half, place = i % 2, i // 2

        def current(j, lanes):
            pieces = []
            for step in steps:
                for block in range(4):
                    at = (half * 4 * (n // 2) + block * (n // 2) + place) * ROWS
                    pieces.append(step[j, at : at + ROWS, lanes])
            return jnp.concatenate(pieces, axis=0)

        queries = []
        for h in range(2):
            lanes = slice(h * HEAD, (h + 1) * HEAD)
            queries.append(current(0, lanes))
            add_keys(queries[h], current(1, lanes), current(2, lanes), sum_ref.at[h], True)
        for g in range(MAXC):

            @pl.when(g < plan_ref[8 + videos[i]])
            def _():
                fetch(i, g).wait()
                for h in range(2):
                    lanes = pl.ds(h * HEAD, HEAD)
                    keys = rms_scale(old_ref[i, g, 0, :, lanes].astype(jnp.float32))
                    add_keys(
                        queries[h],
                        keys.astype(jnp.bfloat16),
                        old_ref[i, g, 1, :, lanes],
                        sum_ref.at[h],
                        False,
                    )

        out = jnp.concatenate(
            [sum_ref[h, :, :HEAD] / sum_ref[h, :, HEAD:] for h in range(2)], axis=1
        ).astype(jnp.bfloat16)
        for step in range(4):
            for block in range(4):
                near, far = (0, -1, 1, 2)[block], sign * step
                a = (y + near if half == 0 else y - far) & 3
                b = (z - far if half == 0 else z + near) & 3
                start = pl.multiple_of((a * 4 + b) * ROWS, ROWS)
                at = (step * 4 + block) * ROWS
                rows_ref[i, pl.ds(start, ROWS), :] = out[at : at + ROWS]
        store(i).start()
    for i in range(n):
        store(i).wait()


def attend(plan, videos, steps, cache, earlier):
    n = len(videos)
    given = [plan, *steps, cache]
    specs = [SMEM] + [VMEM] * 4 + [HBM]
    aliases = {}
    if earlier is not None:
        aliases = {len(given): 0}
        given.append(earlier)
        specs.append(HBM)
    return pl.pallas_call(
        lambda *refs: attend_body(videos, *refs),
        in_specs=specs,
        out_specs=HBM,
        scratch_shapes=[
            pltpu.VMEM((n, MAXC, 2, GROUP, WIDTH), jnp.bfloat16),
            pltpu.VMEM((2, GROUP, 2 * HEAD), jnp.float32),
            pltpu.VMEM((n, GROUP, WIDTH), jnp.bfloat16),
            pltpu.SemaphoreType.DMA((n, MAXC)),
            pltpu.SemaphoreType.DMA((n,)),
        ],
        out_shape=jax.ShapeDtypeStruct((8, GROUP, WIDTH), jnp.bfloat16),
        input_output_aliases=aliases,
        compiler_params=pltpu.CompilerParams(vmem_limit_bytes=12 * MIB),
        cost_estimate=pl.CostEstimate(
            flops=4 * n * 2 * GROUP * 1280 * HEAD,
            bytes_accessed=n * MIB,
            transcendentals=n * 2 * GROUP * 1280,
        ),
        name="attend",
    )(*given)


def ring(dy, dz, odd):
    pairs = []
    for vid in range(8):
        s = odd if vid % 2 else 1
        for y in range(4):
            for z in range(4):
                to = (y + s * dy) % 4 * 4 + (z + s * dz) % 4
                pairs.append((vid * 16 + y * 4 + z, vid * 16 + to))
    return pairs


def send(value, pairs):
    return lax.ppermute(value, ("vid", "fsdp"), pairs)


def after(value, *earlier):
    return lax.optimization_barrier((value, *earlier))[0]


def shards(latents, shift_mod, scale_mod, qkv_weight, kv_cache, holders, cached):
    along_y, along_z = ring(1, 0, -1), ring(0, 1, -1)
    up_y, down_y, up_z, down_z = ring(1, 0, 1), ring(-1, 0, 1), ring(0, 1, 1), ring(0, -1, 1)
    weights = jnp.transpose(qkv_weight, (1, 0, 2))

    halves = slice(0, 2 * ROWS), slice(2 * ROWS, 4 * ROWS)
    own = norm(latents, shift_mod, scale_mod, 2)
    ways = (up_y, down_y), (up_z, down_z)
    near = [[send(rows, way) for way in some] for rows, some in zip(own, ways)]
    far = [
        [send(rows[half], way) for rows, half, way in zip(some, halves, two)]
        for some, two in zip(near, ways)
    ]
    ordered, plan = reorder(holders, cached, kv_cache, *own)
    cache = lax.all_to_all(ordered, "vid", split_axis=0, concat_axis=0, tiled=True)

    sent, projected = [], [[], []]
    groups = [
        [
            [jnp.concatenate([own[i][half], near[i][0][half], near[i][1][half], far[i][g]])]
            for i in range(2)
        ]
        for g, half in enumerate(halves)
    ]
    for step in range(4):
        for g, (a, b) in enumerate(groups):
            if step:
                one, two = a[-1], b[-1]
                if len(sent) >= 2:
                    earlier = projected[g][: step - 1]
                    one = after(one, sent[-2][0], *earlier)
                    two = after(two, sent[-2][1], *earlier)
                sent.append((send(one, along_z), send(two, along_y)))
                a.append(sent[-1][0])
                b.append(sent[-1][1])
        for g, (a, b) in enumerate(groups):
            arrived = [a[-1], b[-1]]
            if step == 3 and g == 1:
                out = attend(plan, (0, 4, 1, 5), projected[0], cache, None)
                arrived = [after(rows, out) for rows in arrived]
            projected[g].append(project(arrived, weights))
    return attend(plan, (2, 6, 3, 7), projected[1], cache, out)


def solution(mesh):
    return jax.shard_map(
        shards,
        mesh=mesh,
        in_specs=(
            P("vid", "fsdp", None),
            P("vid", None),
            P("vid", None),
            P(None, None, "fsdp"),
            P("vid", None, None, None, "fsdp"),
            P(),
            P(),
        ),
        out_specs=P("vid", None, "fsdp"),
        check_vma=False,
    )
```

```python
import math

import jax
import jax.numpy as jnp
from jax import lax
from jax.experimental import pallas as pl
from jax.experimental.pallas import tpu as pltpu
from jax.sharding import PartitionSpec as P

HEAD = 128
GROUP = 256
MAXC = 4
D = 6144
ROWS = 16
WIDTH = 2 * HEAD
SCALE = 1.0 / math.sqrt(HEAD)
HBM = pl.BlockSpec(memory_space=pltpu.HBM)
VMEM = pl.BlockSpec(memory_space=pltpu.VMEM)
SMEM = pl.BlockSpec(memory_space=pltpu.SMEM)
MIB = 1024 * 1024

def rms_scale(values):
    return values * lax.rsqrt(jnp.mean(values * values, axis=-1, keepdims=True) + 1e-06)


def norm_body(count, lat_ref, shift_ref, scale_ref, *refs):
    *outs, in_ref, add_ref, gain_ref, sem = refs
    per = count // len(outs)
    planes = [
        pltpu.make_async_copy(shift_ref, add_ref, sem.at[count]),
        pltpu.make_async_copy(scale_ref, gain_ref, sem.at[count + 1]),
    ]
    rows = [
        pltpu.make_async_copy(lat_ref.at[i], in_ref.at[i], sem.at[i]) for i in range(count)
    ]
    for copy in planes + rows:
        copy.start()
    for copy in planes:
        copy.wait()
    for i in range(count):
        rows[i].wait()
        x = in_ref[i].astype(jnp.float32)
        offsets = x - jnp.mean(x, axis=-1, keepdims=True)
        spread = jnp.mean(offsets * offsets, axis=-1, keepdims=True)
        out = offsets * lax.rsqrt(spread + 1e-06) * (1.0 + gain_ref[i : i + 1]) + add_ref[i : i + 1]
        at = i % per * ROWS
        outs[i // per][at : at + ROWS] = out.astype(jnp.bfloat16)


def norm(latents, shift, scale, parts):
    count = latents.shape[0]
    rows = jax.ShapeDtypeStruct((count // parts * ROWS, D), jnp.bfloat16)
    return pl.pallas_call(
        lambda *refs: norm_body(count, *refs),
        in_specs=[HBM] * 3,
        out_specs=[VMEM] * parts,
        scratch_shapes=[
            pltpu.VMEM((count, ROWS, D), jnp.bfloat16),
            pltpu.VMEM((count, D), jnp.float32),
            pltpu.VMEM((count, D), jnp.float32),
            pltpu.SemaphoreType.DMA((count + 2,)),
        ],
        out_shape=[rows] * parts,
        compiler_params=pltpu.CompilerParams(vmem_limit_bytes=56 * MIB),
        name="norm",
    )(latents, shift, scale)


def reorder_body(count, holders_ref, cached_ref, cache_ref, *refs):
    out_ref, plan_ref, sem = refs[-3:]
    vid, fsdp = lax.axis_index("vid"), lax.axis_index("fsdp")
    loads = []
    for i in range(count):
        slot = jnp.int32(0)
        for v in range(count):
            holder = holders_ref[i * count + v]
            slot = jnp.where((holder >> 3) == vid, holder & 7, slot)
        loads.append(pltpu.make_async_copy(cache_ref.at[slot], out_ref.at[i], sem.at[i]))
        loads[i].start()
    for v in range(count):
        plan_ref[v] = holders_ref[vid * count + v] >> 3
        plan_ref[8 + v] = cached_ref[vid * count + v]
    plan_ref[24] = fsdp >> 2
    plan_ref[25] = fsdp & 3
    plan_ref[26] = vid & 1
    for load in loads:
        load.wait()


def reorder(holders, cached, cache):
    count = cache.shape[0]
    return pl.pallas_call(
        lambda *refs: reorder_body(count, *refs),
        in_specs=[SMEM] * 2 + [HBM],
        out_specs=[VMEM, SMEM],
        scratch_shapes=[pltpu.SemaphoreType.DMA((count,))],
        out_shape=[
            jax.ShapeDtypeStruct(cache.shape, cache.dtype),
            jax.ShapeDtypeStruct((32,), jnp.int32),
        ],
        compiler_params=pltpu.CompilerParams(vmem_limit_bytes=4 * MIB),
        name="reorder",
    )(holders, cached, cache)


def bundle_body(*refs):
    *given, one_ref, two_ref = refs
    for k, ref in enumerate(given):
        half = ref.shape[0] // 2
        one_ref[k * half : (k + 1) * half] = ref[:half]
        two_ref[k * half : (k + 1) * half] = ref[half:]


def bundle(given):
    rows = len(given) * given[0].shape[0] // 2
    return pl.pallas_call(
        bundle_body,
        in_specs=[VMEM] * len(given),
        out_specs=[VMEM] * 2,
        out_shape=[jax.ShapeDtypeStruct((rows, D), jnp.bfloat16)] * 2,
        compiler_params=pltpu.CompilerParams(vmem_limit_bytes=8 * MIB),
        name="bundle",
    )(*given)


PARTS = 4


def project_copies(tokens, w_ref, x_ref, held_ref, sem):
    depth = D // PARTS
    parts = []
    for k in range(PARTS):
        at = pl.ds(k * depth, depth)
        copies = []
        if held_ref is not w_ref:
            copies.append(pltpu.make_async_copy(w_ref.at[:, at], held_ref.at[:, at], sem.at[k, 0]))
        for i, ref in enumerate(tokens):
            rows = ref.shape[0]
            copies.append(
                pltpu.make_async_copy(
                    ref.at[:, at], x_ref.at[pl.ds(i * rows, rows), at], sem.at[k, i + 1]
                )
            )
        parts.append(copies)
    return parts


def project_rows(parts, x_ref, held_ref, out_ref):
    depth = D // PARTS
    totals = [None] * 3
    for k, copies in enumerate(parts):
        for copy in copies:
            copy.wait()
        at = slice(k * depth, (k + 1) * depth)
        x = x_ref[:, at]
        for j in range(3):
            term = jnp.dot(x, held_ref[j, at], preferred_element_type=jnp.float32)
            totals[j] = term if totals[j] is None else totals[j] + term
    for j in range(3):
        for h in range(2):
            values = totals[j][:, h * HEAD : (h + 1) * HEAD]
            if j < 2:
                values = rms_scale(values)
            out_ref[j, :, h * HEAD : (h + 1) * HEAD] = values.astype(jnp.bfloat16)


def project_scratch(count, rows, ready):
    scratch = [pltpu.VMEM((rows, D), jnp.bfloat16), pltpu.SemaphoreType.DMA((PARTS, count + 1))]
    return scratch if ready else [*scratch, pltpu.VMEM((3, D, WIDTH), jnp.bfloat16)]


def project_body(count, *refs):
    tokens, (w_ref, out_ref, x_ref, sem, held_ref) = refs[:count], refs[count:]
    parts = project_copies(tokens, w_ref, x_ref, held_ref, sem)
    for copies in parts:
        for copy in copies:
            copy.start()
    project_rows(parts, x_ref, held_ref, out_ref)


def project(tokens, weights):
    count = len(tokens)
    rows = count * tokens[0].shape[0]
    return pl.pallas_call(
        lambda *refs: project_body(count, *refs),
        in_specs=[HBM] * (count + 1),
        out_specs=VMEM,
        scratch_shapes=project_scratch(count, rows, False),
        out_shape=jax.ShapeDtypeStruct((3, rows, WIDTH), jnp.bfloat16),
        compiler_params=pltpu.CompilerParams(vmem_limit_bytes=56 * MIB),
        cost_estimate=pl.CostEstimate(
            flops=2 * rows * D * 768, bytes_accessed=rows * D * 2, transcendentals=0
        ),
        name="project",
    )(*tokens, weights)


def finish_body(group, videos, ready, plan_ref, *refs):
    n = len(videos)
    steps, tokens, (w_ref, cache_ref) = refs[:3], refs[3:5], refs[5:7]
    out_ref, old_ref, rows_ref, last_ref, in_sem, out_sem, x_ref, sem = refs[-8:]
    held_ref = w_ref
    if not ready:
        out_ref, old_ref, rows_ref, last_ref, in_sem, out_sem, x_ref, sem, held_ref = refs[-9:]
    steps = [*steps, last_ref]
    y, z, core = plan_ref[24], plan_ref[25], plan_ref[26]

    def fetch(i, g):
        place = plan_ref[videos[i]]
        return pltpu.make_async_copy(cache_ref.at[place, g], old_ref.at[i, g], in_sem.at[i, g])

    def store(i):
        return pltpu.make_async_copy(rows_ref.at[i], out_ref.at[videos[i]], out_sem.at[i])

    parts = project_copies(tokens, w_ref, x_ref, held_ref, sem)
    for copies in parts:
        for copy in copies:
            copy.start()
    for i in range(n):
        for g in range(MAXC):

            @pl.when(g < plan_ref[8 + videos[i]])
            def _():
                fetch(i, g).start()

    project_rows(parts, x_ref, held_ref, last_ref)

    def current(i, j, lanes):
        half, place = i // (n // 2), i % (n // 2)
        pieces = []
        for k, step in enumerate(steps):
            first = group * 2 * n * 2 if k < 3 else 0
            for block in range(4):
                at = (first + half * 4 * (n // 2) + block * (n // 2) + place) * ROWS
                pieces.append(step[j, at : at + ROWS, lanes])
        return jnp.concatenate(pieces, axis=0)

    def head(i, live, lanes):
        keys, values = [current(i, 1, lanes)], [current(i, 2, lanes)]
        for g in range(live):
            old = rms_scale(old_ref[i, g, 0, :, lanes].astype(jnp.float32))
            keys.append(old.astype(jnp.bfloat16))
            values.append(old_ref[i, g, 1, :, lanes])
        keys, values = jnp.concatenate(keys, axis=0), jnp.concatenate(values, axis=0)
        logits = lax.dot_general(
            current(i, 0, lanes), keys, (((1,), (1,)), ((), ())), preferred_element_type=jnp.float32
        )
        weights = jnp.exp(logits * SCALE).astype(jnp.bfloat16)
        wide = jnp.concatenate([values, jnp.ones_like(values)], axis=1)
        both = jnp.dot(weights, wide, preferred_element_type=jnp.float32)
        return both[:, :HEAD] / both[:, HEAD:]

    for i in range(n):
        for live in range(1, MAXC + 1):

            @pl.when(plan_ref[8 + videos[i]] == live)
            def _():
                for g in range(live):
                    fetch(i, g).wait()
                out = [head(i, live, slice(h * HEAD, (h + 1) * HEAD)) for h in range(2)]
                out = jnp.concatenate(out, axis=1).astype(jnp.bfloat16)
                for step in range(4):
                    for block in range(4):
                        near, far = (0, -1, 1, 2)[block], -step if i < n // 2 else step
                        a = (y + jnp.where(core == 0, near, far)) & 3
                        b = (z + jnp.where(core == 0, far, near)) & 3
                        start = pl.multiple_of((a * 4 + b) * ROWS, ROWS)
                        at = (step * 4 + block) * ROWS
                        rows_ref[i, pl.ds(start, ROWS), :] = out[at : at + ROWS]

        store(i).start()
    for i in range(n):
        store(i).wait()


def finish(plan, group, videos, steps, tokens, weights, cache, earlier):
    ready = earlier is not None
    n = len(videos)
    rows = 2 * tokens[0].shape[0]
    given = [plan, *steps, *tokens, weights, cache]
    specs = [SMEM] + [VMEM] * 3 + [HBM] * 2 + [VMEM if ready else HBM, HBM]
    aliases = {}
    if earlier is not None:
        aliases = {len(given): 0}
        given.append(earlier)
        specs.append(HBM)
    return pl.pallas_call(
        lambda *refs: finish_body(group, videos, ready, *refs),
        in_specs=specs,
        out_specs=HBM,
        scratch_shapes=[
            pltpu.VMEM((n,) + cache.shape[1:], jnp.bfloat16),
            pltpu.VMEM((n, GROUP, WIDTH), jnp.bfloat16),
            pltpu.VMEM((3, rows, WIDTH), jnp.bfloat16),
            pltpu.SemaphoreType.DMA((n, MAXC)),
            pltpu.SemaphoreType.DMA((n,)),
            *project_scratch(2, rows, ready),
        ],
        out_shape=jax.ShapeDtypeStruct((8, GROUP, WIDTH), jnp.bfloat16),
        input_output_aliases=aliases,
        compiler_params=pltpu.CompilerParams(vmem_limit_bytes=(20 if ready else 36) * MIB),
        cost_estimate=pl.CostEstimate(
            flops=2 * rows * D * 768 + 4 * n * 2 * GROUP * 1280 * HEAD,
            bytes_accessed=n * MIB + rows * D * 2,
            transcendentals=n * 2 * GROUP * 1280,
        ),
        name="finish",
    )(*given)


def ring(phase, step):
    pairs = []
    for vid in range(8):
        for y in range(4):
            for z in range(4):
                if phase == vid % 2:
                    to = (y + step) % 4 * 4 + z
                else:
                    to = y * 4 + (z + step) % 4
                pairs.append((vid * 16 + y * 4 + z, vid * 16 + to))
    return pairs


def send(value, pairs):
    return lax.ppermute(value, ("vid", "fsdp"), pairs)


def after(value, *earlier):
    return lax.optimization_barrier((value, *earlier))[0]


def shards(latents, shift_mod, scale_mod, qkv_weight, kv_cache, holders, cached):
    weights = jnp.transpose(qkv_weight, (1, 0, 2))

    own = norm(latents, shift_mod, scale_mod, 2)
    near = [(send(rows, ring(0, 1)), send(rows, ring(0, -1))) for rows in own]
    ordered, plan = reorder(after(holders, *own), cached, kv_cache)
    far = send(near[0][0], ring(0, 1)), send(near[1][1], ring(0, -1))
    cache = lax.all_to_all(
        after(ordered, *near[0], *near[1], *far), "vid", split_axis=0, concat_axis=0, tiled=True
    )

    groups = [[bundle([rows, *some, last])] for rows, some, last in zip(own, near, far)]
    sent, projected = [], []
    for step in range(4):
        for g, arrived in enumerate(groups):
            if step:
                one, two = arrived[-1]
                if len(sent) >= 2:
                    earlier = projected[: step - 1]
                    one = after(one, sent[-2][0], *earlier)
                    two = after(two, sent[-2][1], *earlier)
                sent.append((send(one, ring(1, 1)), send(two, ring(1, -1))))
                arrived.append(sent[-1])
        if step < 3:
            projected.append(project([*groups[0][-1], *groups[1][-1]], weights))
    out = None
    for g, videos in enumerate(((0, 1, 2, 3), (4, 5, 6, 7))):
        last = groups[g][-1]
        if out is not None:
            last = [after(rows, out) for rows in last]
        out = finish(plan, g, videos, projected, last, weights, cache, out)
    return out


def solution(mesh):
    return jax.shard_map(
        shards,
        mesh=mesh,
        in_specs=(
            P("vid", "fsdp", None),
            P("vid", None),
            P("vid", None),
            P(None, None, "fsdp"),
            P("vid", None, None, None, "fsdp"),
            P(),
            P(),
        ),
        out_specs=P("vid", None, "fsdp"),
        check_vma=False,
    )
```

```python
import math

import jax
import jax.numpy as jnp
from jax import lax
from jax.experimental import pallas as pl
from jax.experimental.pallas import tpu as pltpu
from jax.sharding import PartitionSpec as P

HEAD = 128
GROUP = 256
MAXC = 4
D = 6144
ROWS = 16
WIDTH = 2 * HEAD
SCALE = 1.0 / math.sqrt(HEAD)
HBM = pl.BlockSpec(memory_space=pltpu.HBM)
VMEM = pl.BlockSpec(memory_space=pltpu.VMEM)
SMEM = pl.BlockSpec(memory_space=pltpu.SMEM)
MIB = 1024 * 1024

def rms_scale(values):
    return values * lax.rsqrt(jnp.mean(values * values, axis=-1, keepdims=True) + 1e-06)


def norm_body(count, lat_ref, shift_ref, scale_ref, *refs):
    *outs, in_ref, add_ref, gain_ref, sem = refs
    per = count // len(outs)
    planes = [
        pltpu.make_async_copy(shift_ref, add_ref, sem.at[count]),
        pltpu.make_async_copy(scale_ref, gain_ref, sem.at[count + 1]),
    ]
    rows = [
        pltpu.make_async_copy(lat_ref.at[i], in_ref.at[i], sem.at[i]) for i in range(count)
    ]
    for copy in planes + rows:
        copy.start()
    for copy in planes:
        copy.wait()
    for i in range(count):
        rows[i].wait()
        x = in_ref[i].astype(jnp.float32)
        offsets = x - jnp.mean(x, axis=-1, keepdims=True)
        spread = jnp.mean(offsets * offsets, axis=-1, keepdims=True)
        out = offsets * lax.rsqrt(spread + 1e-06) * (1.0 + gain_ref[i : i + 1]) + add_ref[i : i + 1]
        at = i % per * ROWS
        outs[i // per][at : at + ROWS] = out.astype(jnp.bfloat16)


def norm(latents, shift, scale, parts):
    count = latents.shape[0]
    rows = jax.ShapeDtypeStruct((count // parts * ROWS, D), jnp.bfloat16)
    return pl.pallas_call(
        lambda *refs: norm_body(count, *refs),
        in_specs=[HBM] * 3,
        out_specs=[VMEM] * parts,
        scratch_shapes=[
            pltpu.VMEM((count, ROWS, D), jnp.bfloat16),
            pltpu.VMEM((count, D), jnp.float32),
            pltpu.VMEM((count, D), jnp.float32),
            pltpu.SemaphoreType.DMA((count + 2,)),
        ],
        out_shape=[rows] * parts,
        compiler_params=pltpu.CompilerParams(vmem_limit_bytes=56 * MIB),
        name="norm",
    )(latents, shift, scale)


def reorder_body(count, holders_ref, cached_ref, cache_ref, *refs):
    out_ref, plan_ref, sem = refs[-3:]
    vid, fsdp = lax.axis_index("vid"), lax.axis_index("fsdp")
    loads = []
    for i in range(count):
        slot = jnp.int32(0)
        for v in range(count):
            holder = holders_ref[i * count + v]
            slot = jnp.where((holder >> 3) == vid, holder & 7, slot)
        loads.append(pltpu.make_async_copy(cache_ref.at[slot], out_ref.at[i], sem.at[i]))
        loads[i].start()
    for v in range(count):
        plan_ref[v] = holders_ref[vid * count + v] >> 3
        plan_ref[8 + v] = cached_ref[vid * count + v]
    plan_ref[24] = fsdp >> 2
    plan_ref[25] = fsdp & 3
    plan_ref[26] = vid & 1
    for load in loads:
        load.wait()


def reorder(holders, cached, cache):
    count = cache.shape[0]
    return pl.pallas_call(
        lambda *refs: reorder_body(count, *refs),
        in_specs=[SMEM] * 2 + [HBM],
        out_specs=[VMEM, SMEM],
        scratch_shapes=[pltpu.SemaphoreType.DMA((count,))],
        out_shape=[
            jax.ShapeDtypeStruct(cache.shape, cache.dtype),
            jax.ShapeDtypeStruct((32,), jnp.int32),
        ],
        compiler_params=pltpu.CompilerParams(vmem_limit_bytes=4 * MIB),
        name="reorder",
    )(holders, cached, cache)


def bundle_body(*refs):
    *given, one_ref, two_ref = refs
    for k, ref in enumerate(given):
        half = ref.shape[0] // 2
        one_ref[k * half : (k + 1) * half] = ref[:half]
        two_ref[k * half : (k + 1) * half] = ref[half:]


def bundle(given):
    rows = len(given) * given[0].shape[0] // 2
    return pl.pallas_call(
        bundle_body,
        in_specs=[VMEM] * len(given),
        out_specs=[VMEM] * 2,
        out_shape=[jax.ShapeDtypeStruct((rows, D), jnp.bfloat16)] * 2,
        compiler_params=pltpu.CompilerParams(vmem_limit_bytes=8 * MIB),
        cost_estimate=pl.CostEstimate(flops=50_000_000_000, bytes_accessed=0, transcendentals=0),
        name="bundle",
    )(*given)


PARTS = 4


def project_copies(tokens, w_ref, x_ref, held_ref, sem):
    depth = D // PARTS
    parts = []
    for k in range(PARTS):
        at = pl.ds(k * depth, depth)
        copies = []
        if held_ref is not w_ref:
            copies.append(pltpu.make_async_copy(w_ref.at[:, at], held_ref.at[:, at], sem.at[k, 0]))
        for i, ref in enumerate(tokens):
            rows = ref.shape[0]
            copies.append(
                pltpu.make_async_copy(
                    ref.at[:, at], x_ref.at[pl.ds(i * rows, rows), at], sem.at[k, i + 1]
                )
            )
        parts.append(copies)
    return parts


def project_rows(parts, x_ref, held_ref, out_ref):
    depth = D // PARTS
    totals = [None] * 3
    for k, copies in enumerate(parts):
        for copy in copies:
            copy.wait()
        at = slice(k * depth, (k + 1) * depth)
        x = x_ref[:, at]
        for j in range(3):
            term = jnp.dot(x, held_ref[j, at], preferred_element_type=jnp.float32)
            totals[j] = term if totals[j] is None else totals[j] + term
    for j in range(3):
        for h in range(2):
            values = totals[j][:, h * HEAD : (h + 1) * HEAD]
            if j < 2:
                values = rms_scale(values)
            out_ref[j, :, h * HEAD : (h + 1) * HEAD] = values.astype(jnp.bfloat16)


def project_scratch(count, rows, ready):
    scratch = [pltpu.VMEM((rows, D), jnp.bfloat16), pltpu.SemaphoreType.DMA((PARTS, count + 1))]
    return scratch if ready else [*scratch, pltpu.VMEM((3, D, WIDTH), jnp.bfloat16)]


def project_body(count, *refs):
    tokens, (w_ref, out_ref, x_ref, sem, held_ref) = refs[:count], refs[count:]
    parts = project_copies(tokens, w_ref, x_ref, held_ref, sem)
    for copies in parts:
        for copy in copies:
            copy.start()
    project_rows(parts, x_ref, held_ref, out_ref)


def project(tokens, weights):
    count = len(tokens)
    rows = count * tokens[0].shape[0]
    return pl.pallas_call(
        lambda *refs: project_body(count, *refs),
        in_specs=[HBM] * (count + 1),
        out_specs=VMEM,
        scratch_shapes=project_scratch(count, rows, False),
        out_shape=jax.ShapeDtypeStruct((3, rows, WIDTH), jnp.bfloat16),
        compiler_params=pltpu.CompilerParams(vmem_limit_bytes=56 * MIB),
        cost_estimate=pl.CostEstimate(
            flops=2 * rows * D * 768, bytes_accessed=rows * D * 2, transcendentals=0
        ),
        name="project",
    )(*tokens, weights)


def finish_body(group, videos, ready, plan_ref, *refs):
    n = len(videos)
    steps, tokens, (w_ref, cache_ref) = refs[:3], refs[3:5], refs[5:7]
    scratch, held_ref = refs[-10:], w_ref
    if not ready:
        scratch, held_ref = refs[-11:-1], refs[-1]
    out_ref, old_ref, rows_ref, last_ref, step_ref, in_sem, out_sem, step_sem, x_ref, sem = scratch
    size = last_ref.shape[1]
    y, z, core = plan_ref[24], plan_ref[25], plan_ref[26]

    def fetch(i, g):
        place = plan_ref[videos[i]]
        return pltpu.make_async_copy(cache_ref.at[place, g], old_ref.at[i, g], in_sem.at[i, g])

    def store(i):
        return pltpu.make_async_copy(rows_ref.at[i], out_ref.at[videos[i]], out_sem.at[i])

    parts = project_copies(tokens, w_ref, x_ref, held_ref, sem)
    for copies in parts:
        for copy in copies:
            copy.start()
    for i in range(n):
        for g in range(MAXC):

            @pl.when(g < plan_ref[8 + videos[i]])
            def _():
                fetch(i, g).start()

    fetched = [
        pltpu.make_async_copy(
            step.at[:, pl.ds(group * size, size)], step_ref.at[k], step_sem.at[k]
        )
        for k, step in enumerate(steps)
    ]
    for copy in fetched:
        copy.start()

    project_rows(parts, x_ref, held_ref, last_ref)
    for copy in fetched:
        copy.wait()

    def current(i, j, lanes):
        half, place = i // (n // 2), i % (n // 2)
        pieces = []
        for step in (*(step_ref.at[k] for k in range(3)), last_ref):
            for block in range(4):
                at = (half * 4 * (n // 2) + block * (n // 2) + place) * ROWS
                pieces.append(step[j, at : at + ROWS, lanes])
        return jnp.concatenate(pieces, axis=0)

    def head(i, live, lanes):
        keys, values = [current(i, 1, lanes)], [current(i, 2, lanes)]
        for g in range(live):
            old = rms_scale(old_ref[i, g, 0, :, lanes].astype(jnp.float32))
            keys.append(old.astype(jnp.bfloat16))
            values.append(old_ref[i, g, 1, :, lanes])
        keys, values = jnp.concatenate(keys, axis=0), jnp.concatenate(values, axis=0)
        logits = lax.dot_general(
            current(i, 0, lanes), keys, (((1,), (1,)), ((), ())), preferred_element_type=jnp.float32
        )
        weights = jnp.exp(logits * SCALE).astype(jnp.bfloat16)
        wide = jnp.concatenate([values, jnp.ones_like(values)], axis=1)
        both = jnp.dot(weights, wide, preferred_element_type=jnp.float32)
        return both[:, :HEAD] / both[:, HEAD:]

    for i in range(n):
        for live in range(1, MAXC + 1):

            @pl.when(plan_ref[8 + videos[i]] == live)
            def _():
                for g in range(live):
                    fetch(i, g).wait()
                out = [head(i, live, slice(h * HEAD, (h + 1) * HEAD)) for h in range(2)]
                out = jnp.concatenate(out, axis=1).astype(jnp.bfloat16)
                for step in range(4):
                    for block in range(4):
                        near, far = (0, -1, 1, 2)[block], -step if i < n // 2 else step
                        a = (y + jnp.where(core == 0, near, far)) & 3
                        b = (z + jnp.where(core == 0, far, near)) & 3
                        start = pl.multiple_of((a * 4 + b) * ROWS, ROWS)
                        at = (step * 4 + block) * ROWS
                        rows_ref[i, pl.ds(start, ROWS), :] = out[at : at + ROWS]

        store(i).start()
    for i in range(n):
        store(i).wait()


def finish(plan, group, videos, steps, tokens, weights, cache, earlier):
    ready = earlier is not None
    n = len(videos)
    rows = 2 * tokens[0].shape[0]
    given = [plan, *steps, *tokens, weights, cache]
    specs = [SMEM] + [HBM] * 5 + [VMEM if ready else HBM, HBM]
    aliases = {}
    if earlier is not None:
        aliases = {len(given): 0}
        given.append(earlier)
        specs.append(HBM)
    return pl.pallas_call(
        lambda *refs: finish_body(group, videos, ready, *refs),
        in_specs=specs,
        out_specs=HBM,
        scratch_shapes=[
            pltpu.VMEM((n,) + cache.shape[1:], jnp.bfloat16),
            pltpu.VMEM((n, GROUP, WIDTH), jnp.bfloat16),
            pltpu.VMEM((3, rows, WIDTH), jnp.bfloat16),
            pltpu.VMEM((3, 3, rows, WIDTH), jnp.bfloat16),
            pltpu.SemaphoreType.DMA((n, MAXC)),
            pltpu.SemaphoreType.DMA((n,)),
            pltpu.SemaphoreType.DMA((3,)),
            *project_scratch(2, rows, ready),
        ],
        out_shape=jax.ShapeDtypeStruct((8, GROUP, WIDTH), jnp.bfloat16),
        input_output_aliases=aliases,
        compiler_params=pltpu.CompilerParams(vmem_limit_bytes=(20 if ready else 50) * MIB),
        cost_estimate=pl.CostEstimate(
            flops=2 * rows * D * 768 + 4 * n * 2 * GROUP * 1280 * HEAD,
            bytes_accessed=n * MIB + rows * D * 2,
            transcendentals=n * 2 * GROUP * 1280,
        ),
        name="finish",
    )(*given)


def ring(phase, step):
    pairs = []
    for vid in range(8):
        for y in range(4):
            for z in range(4):
                if phase == vid % 2:
                    to = (y + step) % 4 * 4 + z
                else:
                    to = y * 4 + (z + step) % 4
                pairs.append((vid * 16 + y * 4 + z, vid * 16 + to))
    return pairs


def send(value, pairs):
    return lax.ppermute(value, ("vid", "fsdp"), pairs)


def after(value, *earlier):
    return lax.optimization_barrier((value, *earlier))[0]


def shards(latents, shift_mod, scale_mod, qkv_weight, kv_cache, holders, cached):
    weights = jnp.transpose(qkv_weight, (1, 0, 2))

    own = norm(latents, shift_mod, scale_mod, 2)
    below, above = send(own[0], ring(0, 1)), send(own[1], ring(0, -1))
    near = [
        (below, send(after(own[0], below), ring(0, -1))),
        (send(after(own[1], above), ring(0, 1)), above),
    ]
    ordered, plan = reorder(after(holders, below, above), cached, kv_cache)
    far = send(below, ring(0, 1)), send(above, ring(0, -1))
    far = after(far[0], far[1]), far[1]
    cache = lax.all_to_all(
        ordered, "vid", split_axis=0, concat_axis=0, tiled=True
    )

    groups = [[bundle([rows, *some, last])] for rows, some, last in zip(own, near, far)]
    sent, projected = [], []
    for step in range(4):
        for g, arrived in enumerate(groups):
            if step:
                one, two = arrived[-1]
                if len(sent) >= 2:
                    earlier = projected[: step - 1]
                    one = after(one, sent[-2][0], *earlier)
                    two = after(two, sent[-2][1], *earlier)
                sent.append((send(one, ring(1, 1)), send(two, ring(1, -1))))
                arrived.append(sent[-1])
        if step < 3:
            projected.append(project([*groups[0][-1], *groups[1][-1]], weights))
    out = None
    for g, videos in enumerate(((0, 1, 2, 3), (4, 5, 6, 7))):
        last = groups[g][-1]
        if out is not None:
            last = [after(rows, out) for rows in last]
        out = finish(plan, g, videos, projected, last, weights, cache, out)
    return out


def solution(mesh):
    return jax.shard_map(
        shards,
        mesh=mesh,
        in_specs=(
            P("vid", "fsdp", None),
            P("vid", None),
            P("vid", None),
            P(None, None, "fsdp"),
            P("vid", None, None, None, "fsdp"),
            P(),
            P(),
        ),
        out_specs=P("vid", None, "fsdp"),
        check_vma=False,
    )
```

```python
import math

import jax
import jax.numpy as jnp
from jax import lax
from jax.experimental import pallas as pl
from jax.experimental.pallas import tpu as pltpu
from jax.sharding import PartitionSpec as P

HEAD = 128
GROUP = 256
MAXC = 4
D = 6144
ROWS = 16
WIDTH = 2 * HEAD
SCALE = 1.0 / math.sqrt(HEAD)
HBM = pl.BlockSpec(memory_space=pltpu.HBM)
VMEM = pl.BlockSpec(memory_space=pltpu.VMEM)
SMEM = pl.BlockSpec(memory_space=pltpu.SMEM)
MIB = 1024 * 1024
BLOCK = 512

def rms_scale(values):
    return values * lax.rsqrt(jnp.mean(values * values, axis=-1, keepdims=True) + 1e-06)


def norm_body(count, lat_ref, shift_ref, scale_ref, *refs):
    *outs, in_ref, add_ref, gain_ref, held_ref, sem, out_sem = refs
    per = count // len(outs)
    planes = [
        pltpu.make_async_copy(shift_ref, add_ref, sem.at[count]),
        pltpu.make_async_copy(scale_ref, gain_ref, sem.at[count + 1]),
    ]
    rows = [
        pltpu.make_async_copy(lat_ref.at[i], in_ref.at[i], sem.at[i]) for i in range(count)
    ]
    stores = [
        pltpu.make_async_copy(
            held_ref.at[i], outs[i // per].at[pl.ds(i % per * ROWS, ROWS)], out_sem.at[i]
        )
        for i in range(count)
    ]
    for copy in planes + rows:
        copy.start()
    for copy in planes:
        copy.wait()
    for i in range(count):
        rows[i].wait()
        blocks = [slice(k, k + BLOCK) for k in range(0, D, BLOCK)]

        def mean(of):
            total = of(blocks[0])
            for block in blocks[1:]:
                total = total + of(block)
            return jnp.sum(total, axis=-1, keepdims=True) * (1.0 / D)

        center = mean(lambda block: in_ref[i, :, block].astype(jnp.float32))
        spread = mean(lambda block: (in_ref[i, :, block].astype(jnp.float32) - center) ** 2)
        inverse = lax.rsqrt(spread + 1e-06)
        for block in blocks:
            offsets = in_ref[i, :, block].astype(jnp.float32) - center
            gain, shift = 1.0 + gain_ref[i : i + 1, block], add_ref[i : i + 1, block]
            held_ref[i, :, block] = (offsets * inverse * gain + shift).astype(jnp.bfloat16)
        stores[i].start()
    for store in stores:
        store.wait()


def norm(latents, shift, scale, parts):
    count = latents.shape[0]
    rows = jax.ShapeDtypeStruct((count // parts * ROWS, D), jnp.bfloat16)
    return pl.pallas_call(
        lambda *refs: norm_body(count, *refs),
        in_specs=[HBM] * 3,
        out_specs=[HBM] * parts,
        scratch_shapes=[
            pltpu.VMEM((count, ROWS, D), jnp.bfloat16),
            pltpu.VMEM((count, D), jnp.float32),
            pltpu.VMEM((count, D), jnp.float32),
            pltpu.VMEM((count, ROWS, D), jnp.bfloat16),
            pltpu.SemaphoreType.DMA((count + 2,)),
            pltpu.SemaphoreType.DMA((count,)),
        ],
        out_shape=[rows] * parts,
        compiler_params=pltpu.CompilerParams(vmem_limit_bytes=56 * MIB),
        name="norm",
    )(latents, shift, scale)


def reorder_body(count, holders_ref, cached_ref, cache_ref, *refs):
    out_ref, plan_ref, sem = refs[-3:]
    vid, fsdp = lax.axis_index("vid"), lax.axis_index("fsdp")
    loads = []
    for i in range(count):
        slot = jnp.int32(0)
        for v in range(count):
            holder = holders_ref[i * count + v]
            slot = jnp.where((holder >> 3) == vid, holder & 7, slot)
        loads.append(pltpu.make_async_copy(cache_ref.at[slot], out_ref.at[i], sem.at[i]))
        loads[i].start()
    for v in range(count):
        plan_ref[v] = holders_ref[vid * count + v] >> 3
        plan_ref[8 + v] = cached_ref[vid * count + v]
    plan_ref[24] = fsdp >> 2
    plan_ref[25] = fsdp & 3
    plan_ref[26] = vid & 1
    for load in loads:
        load.wait()


def reorder(holders, cached, cache):
    count = cache.shape[0]
    return pl.pallas_call(
        lambda *refs: reorder_body(count, *refs),
        in_specs=[SMEM] * 2 + [HBM],
        out_specs=[VMEM, SMEM],
        scratch_shapes=[pltpu.SemaphoreType.DMA((count,))],
        out_shape=[
            jax.ShapeDtypeStruct(cache.shape, cache.dtype),
            jax.ShapeDtypeStruct((32,), jnp.int32),
        ],
        compiler_params=pltpu.CompilerParams(vmem_limit_bytes=4 * MIB),
        name="reorder",
    )(holders, cached, cache)


def bundle_body(*refs):
    *given, one_ref, two_ref = refs
    for k, ref in enumerate(given):
        half = ref.shape[0] // 2
        one_ref[k * half : (k + 1) * half] = ref[:half]
        two_ref[k * half : (k + 1) * half] = ref[half:]


def bundle(given):
    rows = len(given) * given[0].shape[0] // 2
    return pl.pallas_call(
        bundle_body,
        in_specs=[VMEM] * len(given),
        out_specs=[VMEM] * 2,
        out_shape=[jax.ShapeDtypeStruct((rows, D), jnp.bfloat16)] * 2,
        compiler_params=pltpu.CompilerParams(vmem_limit_bytes=8 * MIB),
        cost_estimate=pl.CostEstimate(flops=50_000_000_000, bytes_accessed=0, transcendentals=0),
        name="bundle",
    )(*given)


PARTS = 4


def project_copies(tokens, w_ref, x_ref, held_ref, sem):
    depth = D // PARTS
    parts = []
    for k in range(PARTS):
        at = pl.ds(k * depth, depth)
        copies = []
        if held_ref is not w_ref:
            copies.append(pltpu.make_async_copy(w_ref.at[:, at], held_ref.at[:, at], sem.at[k, 0]))
        for i, ref in enumerate(tokens):
            rows = ref.shape[0]
            copies.append(
                pltpu.make_async_copy(
                    ref.at[:, at], x_ref.at[pl.ds(i * rows, rows), at], sem.at[k, i + 1]
                )
            )
        parts.append(copies)
    return parts


def project_rows(parts, x_ref, held_ref, out_ref):
    depth = D // PARTS
    totals = [None] * 3
    for k, copies in enumerate(parts):
        for copy in copies:
            copy.wait()
        at = slice(k * depth, (k + 1) * depth)
        x = x_ref[:, at]
        for j in range(3):
            term = jnp.dot(x, held_ref[j, at], preferred_element_type=jnp.float32)
            totals[j] = term if totals[j] is None else totals[j] + term
    for j in range(3):
        for h in range(2):
            values = totals[j][:, h * HEAD : (h + 1) * HEAD]
            if j < 2:
                values = rms_scale(values)
            out_ref[j, :, h * HEAD : (h + 1) * HEAD] = values.astype(jnp.bfloat16)


def project_scratch(count, rows, ready):
    scratch = [pltpu.VMEM((rows, D), jnp.bfloat16), pltpu.SemaphoreType.DMA((PARTS, count + 1))]
    return scratch if ready else [*scratch, pltpu.VMEM((3, D, WIDTH), jnp.bfloat16)]


def project_body(count, *refs):
    tokens, (w_ref, out_ref, x_ref, sem, held_ref) = refs[:count], refs[count:]
    parts = project_copies(tokens, w_ref, x_ref, held_ref, sem)
    for copies in parts:
        for copy in copies:
            copy.start()
    project_rows(parts, x_ref, held_ref, out_ref)


def project(tokens, weights):
    count = len(tokens)
    rows = count * tokens[0].shape[0]
    return pl.pallas_call(
        lambda *refs: project_body(count, *refs),
        in_specs=[HBM] * (count + 1),
        out_specs=VMEM,
        scratch_shapes=project_scratch(count, rows, False),
        out_shape=jax.ShapeDtypeStruct((3, rows, WIDTH), jnp.bfloat16),
        compiler_params=pltpu.CompilerParams(vmem_limit_bytes=56 * MIB),
        cost_estimate=pl.CostEstimate(
            flops=2 * rows * D * 768, bytes_accessed=rows * D * 2, transcendentals=0
        ),
        name="project",
    )(*tokens, weights)


def finish_body(group, videos, ready, plan_ref, *refs):
    n = len(videos)
    steps, tokens, (w_ref, cache_ref) = refs[:3], refs[3:5], refs[5:7]
    scratch, held_ref = refs[-10:], w_ref
    if not ready:
        scratch, held_ref = refs[-11:-1], refs[-1]
    out_ref, old_ref, rows_ref, last_ref, step_ref, in_sem, out_sem, step_sem, x_ref, sem = scratch
    size = last_ref.shape[1]
    y, z, core = plan_ref[24], plan_ref[25], plan_ref[26]

    def fetch(i, g):
        place = plan_ref[videos[i]]
        return pltpu.make_async_copy(cache_ref.at[place, g], old_ref.at[i, g], in_sem.at[i, g])

    def store(i):
        return pltpu.make_async_copy(rows_ref.at[i], out_ref.at[videos[i]], out_sem.at[i])

    parts = project_copies(tokens, w_ref, x_ref, held_ref, sem)
    for copies in parts:
        for copy in copies:
            copy.start()
    for i in range(n):
        for g in range(MAXC):

            @pl.when(g < plan_ref[8 + videos[i]])
            def _():
                fetch(i, g).start()

    fetched = [
        pltpu.make_async_copy(
            step.at[:, pl.ds(group * size, size)], step_ref.at[k], step_sem.at[k]
        )
        for k, step in enumerate(steps)
    ]
    for copy in fetched:
        copy.start()

    project_rows(parts, x_ref, held_ref, last_ref)
    for copy in fetched:
        copy.wait()

    def current(i, j, lanes):
        half, place = i // (n // 2), i % (n // 2)
        pieces = []
        for step in (*(step_ref.at[k] for k in range(3)), last_ref):
            for block in range(4):
                at = (half * 4 * (n // 2) + block * (n // 2) + place) * ROWS
                pieces.append(step[j, at : at + ROWS, lanes])
        return jnp.concatenate(pieces, axis=0)

    def head(i, live, lanes):
        keys, values = [current(i, 1, lanes)], [current(i, 2, lanes)]
        for g in range(live):
            old = rms_scale(old_ref[i, g, 0, :, lanes].astype(jnp.float32))
            keys.append(old.astype(jnp.bfloat16))
            values.append(old_ref[i, g, 1, :, lanes])
        keys, values = jnp.concatenate(keys, axis=0), jnp.concatenate(values, axis=0)
        logits = lax.dot_general(
            current(i, 0, lanes), keys, (((1,), (1,)), ((), ())), preferred_element_type=jnp.float32
        )
        weights = jnp.exp(logits * SCALE).astype(jnp.bfloat16)
        wide = jnp.concatenate([values, jnp.ones_like(values)], axis=1)
        both = jnp.dot(weights, wide, preferred_element_type=jnp.float32)
        return both[:, :HEAD] / both[:, HEAD:]

    for i in range(n):
        for live in range(1, MAXC + 1):

            @pl.when(plan_ref[8 + videos[i]] == live)
            def _():
                for g in range(live):
                    fetch(i, g).wait()
                out = [head(i, live, slice(h * HEAD, (h + 1) * HEAD)) for h in range(2)]
                out = jnp.concatenate(out, axis=1).astype(jnp.bfloat16)
                for step in range(4):
                    for block in range(4):
                        near, far = (0, -1, 1, 2)[block], -step if i < n // 2 else step
                        a = (y + jnp.where(core == 0, near, far)) & 3
                        b = (z + jnp.where(core == 0, far, near)) & 3
                        start = pl.multiple_of((a * 4 + b) * ROWS, ROWS)
                        at = (step * 4 + block) * ROWS
                        rows_ref[i, pl.ds(start, ROWS), :] = out[at : at + ROWS]

        store(i).start()
    for i in range(n):
        store(i).wait()


def finish(plan, group, videos, steps, tokens, weights, cache, earlier):
    ready = earlier is not None
    n = len(videos)
    rows = 2 * tokens[0].shape[0]
    given = [plan, *steps, *tokens, weights, cache]
    specs = [SMEM] + [HBM] * 5 + [VMEM if ready else HBM, HBM]
    aliases = {}
    if earlier is not None:
        aliases = {len(given): 0}
        given.append(earlier)
        specs.append(HBM)
    return pl.pallas_call(
        lambda *refs: finish_body(group, videos, ready, *refs),
        in_specs=specs,
        out_specs=HBM,
        scratch_shapes=[
            pltpu.VMEM((n,) + cache.shape[1:], jnp.bfloat16),
            pltpu.VMEM((n, GROUP, WIDTH), jnp.bfloat16),
            pltpu.VMEM((3, rows, WIDTH), jnp.bfloat16),
            pltpu.VMEM((3, 3, rows, WIDTH), jnp.bfloat16),
            pltpu.SemaphoreType.DMA((n, MAXC)),
            pltpu.SemaphoreType.DMA((n,)),
            pltpu.SemaphoreType.DMA((3,)),
            *project_scratch(2, rows, ready),
        ],
        out_shape=jax.ShapeDtypeStruct((8, GROUP, WIDTH), jnp.bfloat16),
        input_output_aliases=aliases,
        compiler_params=pltpu.CompilerParams(vmem_limit_bytes=(20 if ready else 50) * MIB),
        cost_estimate=pl.CostEstimate(
            flops=2 * rows * D * 768 + 4 * n * 2 * GROUP * 1280 * HEAD,
            bytes_accessed=n * MIB + rows * D * 2,
            transcendentals=n * 2 * GROUP * 1280,
        ),
        name="finish",
    )(*given)


def ring(phase, step):
    pairs = []
    for vid in range(8):
        for y in range(4):
            for z in range(4):
                if phase == vid % 2:
                    to = (y + step) % 4 * 4 + z
                else:
                    to = y * 4 + (z + step) % 4
                pairs.append((vid * 16 + y * 4 + z, vid * 16 + to))
    return pairs


def send(value, pairs):
    return lax.ppermute(value, ("vid", "fsdp"), pairs)


def after(value, *earlier):
    return lax.optimization_barrier((value, *earlier))[0]


def shards(latents, shift_mod, scale_mod, qkv_weight, kv_cache, holders, cached):
    weights = jnp.transpose(qkv_weight, (1, 0, 2))

    own = norm(latents, shift_mod, scale_mod, 2)
    below, above = send(own[0], ring(0, 1)), send(own[1], ring(0, -1))
    near = [
        (below, send(after(own[0], below), ring(0, -1))),
        (send(after(own[1], above), ring(0, 1)), above),
    ]
    ordered, plan = reorder(after(holders, below, above), cached, kv_cache)
    far = send(below, ring(0, 1)), send(above, ring(0, -1))
    far = after(far[0], far[1]), far[1]
    cache = lax.all_to_all(
        ordered, "vid", split_axis=0, concat_axis=0, tiled=True
    )

    groups = [[bundle([rows, *some, last])] for rows, some, last in zip(own, near, far)]
    sent, projected = [], []
    for step in range(4):
        for g, arrived in enumerate(groups):
            if step:
                one, two = arrived[-1]
                if len(sent) >= 2:
                    earlier = projected[: step - 1]
                    one = after(one, sent[-2][0], *earlier)
                    two = after(two, sent[-2][1], *earlier)
                sent.append((send(one, ring(1, 1)), send(two, ring(1, -1))))
                arrived.append(sent[-1])
        if step < 3:
            projected.append(project([*groups[0][-1], *groups[1][-1]], weights))
    out = None
    for g, videos in enumerate(((0, 1, 2, 3), (4, 5, 6, 7))):
        last = groups[g][-1]
        if out is not None:
            last = [after(rows, out) for rows in last]
        out = finish(plan, g, videos, projected, last, weights, cache, out)
    return out


def solution(mesh):
    return jax.shard_map(
        shards,
        mesh=mesh,
        in_specs=(
            P("vid", "fsdp", None),
            P("vid", None),
            P("vid", None),
            P(None, None, "fsdp"),
            P("vid", None, None, None, "fsdp"),
            P(),
            P(),
        ),
        out_specs=P("vid", None, "fsdp"),
        check_vma=False,
    )
```

```python
import math

import jax
import jax.numpy as jnp
from jax import lax
from jax.experimental import pallas as pl
from jax.experimental.pallas import tpu as pltpu
from jax.sharding import PartitionSpec as P

HEAD = 128
GROUP = 256
MAXC = 4
D = 6144
ROWS = 16
WIDTH = 2 * HEAD
SCALE = math.log2(math.e) / math.sqrt(HEAD)
HBM = pl.BlockSpec(memory_space=pltpu.HBM)
VMEM = pl.BlockSpec(memory_space=pltpu.VMEM)
SMEM = pl.BlockSpec(memory_space=pltpu.SMEM)
MIB = 1024 * 1024
BLOCK = 512

def rms_scale(values):
    return values * lax.rsqrt(jnp.mean(values * values, axis=-1, keepdims=True) + 1e-06)


def norm_body(count, lat_ref, shift_ref, scale_ref, *refs):
    *outs, in_ref, add_ref, gain_ref, held_ref, sem, out_sem = refs
    per = count // len(outs)
    planes = [
        pltpu.make_async_copy(shift_ref, add_ref, sem.at[count]),
        pltpu.make_async_copy(scale_ref, gain_ref, sem.at[count + 1]),
    ]
    rows = [
        pltpu.make_async_copy(lat_ref.at[i], in_ref.at[i], sem.at[i]) for i in range(count)
    ]
    stores = [
        pltpu.make_async_copy(
            held_ref.at[i], outs[i // per].at[pl.ds(i % per * ROWS, ROWS)], out_sem.at[i]
        )
        for i in range(count)
    ]
    for copy in planes + rows:
        copy.start()
    for copy in planes:
        copy.wait()
    for i in range(count):
        rows[i].wait()
        blocks = [slice(k, k + BLOCK) for k in range(0, D, BLOCK)]

        def mean(of):
            total = of(blocks[0])
            for block in blocks[1:]:
                total = total + of(block)
            return jnp.sum(total, axis=-1, keepdims=True) * (1.0 / D)

        center = mean(lambda block: in_ref[i, :, block].astype(jnp.float32))
        spread = mean(lambda block: (in_ref[i, :, block].astype(jnp.float32) - center) ** 2)
        inverse = lax.rsqrt(spread + 1e-06)
        for block in blocks:
            offsets = in_ref[i, :, block].astype(jnp.float32) - center
            gain, shift = 1.0 + gain_ref[i : i + 1, block], add_ref[i : i + 1, block]
            held_ref[i, :, block] = (offsets * inverse * gain + shift).astype(jnp.bfloat16)
        stores[i].start()
    for store in stores:
        store.wait()


def norm(latents, shift, scale, parts):
    count = latents.shape[0]
    rows = jax.ShapeDtypeStruct((count // parts * ROWS, D), jnp.bfloat16)
    return pl.pallas_call(
        lambda *refs: norm_body(count, *refs),
        in_specs=[HBM] * 3,
        out_specs=[HBM] * parts,
        scratch_shapes=[
            pltpu.VMEM((count, ROWS, D), jnp.bfloat16),
            pltpu.VMEM((count, D), jnp.float32),
            pltpu.VMEM((count, D), jnp.float32),
            pltpu.VMEM((count, ROWS, D), jnp.bfloat16),
            pltpu.SemaphoreType.DMA((count + 2,)),
            pltpu.SemaphoreType.DMA((count,)),
        ],
        out_shape=[rows] * parts,
        compiler_params=pltpu.CompilerParams(vmem_limit_bytes=56 * MIB),
        name="norm",
    )(latents, shift, scale)


def reorder_body(count, holders_ref, cached_ref, cache_ref, *refs):
    out_ref, plan_ref, sem = refs[-3:]
    vid, fsdp = lax.axis_index("vid"), lax.axis_index("fsdp")
    loads = []
    for i in range(count):
        slot = jnp.int32(0)
        for v in range(count):
            holder = holders_ref[i * count + v]
            slot = jnp.where((holder >> 3) == vid, holder & 7, slot)
        loads.append(pltpu.make_async_copy(cache_ref.at[slot], out_ref.at[i], sem.at[i]))
        loads[i].start()
    for v in range(count):
        plan_ref[v] = holders_ref[vid * count + v] >> 3
        plan_ref[8 + v] = cached_ref[vid * count + v]
    plan_ref[24] = fsdp >> 2
    plan_ref[25] = fsdp & 3
    plan_ref[26] = vid & 1
    for load in loads:
        load.wait()


def reorder(holders, cached, cache):
    count = cache.shape[0]
    return pl.pallas_call(
        lambda *refs: reorder_body(count, *refs),
        in_specs=[SMEM] * 2 + [HBM],
        out_specs=[VMEM, SMEM],
        scratch_shapes=[pltpu.SemaphoreType.DMA((count,))],
        out_shape=[
            jax.ShapeDtypeStruct(cache.shape, cache.dtype),
            jax.ShapeDtypeStruct((32,), jnp.int32),
        ],
        compiler_params=pltpu.CompilerParams(vmem_limit_bytes=4 * MIB),
        name="reorder",
    )(holders, cached, cache)


def bundle_body(*refs):
    *given, one_ref, two_ref = refs
    for k, ref in enumerate(given):
        half = ref.shape[0] // 2
        one_ref[k * half : (k + 1) * half] = ref[:half]
        two_ref[k * half : (k + 1) * half] = ref[half:]


def bundle(given):
    rows = len(given) * given[0].shape[0] // 2
    return pl.pallas_call(
        bundle_body,
        in_specs=[VMEM] * len(given),
        out_specs=[VMEM] * 2,
        out_shape=[jax.ShapeDtypeStruct((rows, D), jnp.bfloat16)] * 2,
        compiler_params=pltpu.CompilerParams(vmem_limit_bytes=8 * MIB),
        cost_estimate=pl.CostEstimate(flops=50_000_000_000, bytes_accessed=0, transcendentals=0),
        name="bundle",
    )(*given)


PARTS = 4


def project_copies(tokens, w_ref, x_ref, held_ref, sem):
    depth = D // PARTS
    parts = []
    for k in range(PARTS):
        at = pl.ds(k * depth, depth)
        copies = []
        if held_ref is not w_ref:
            copies.append(pltpu.make_async_copy(w_ref.at[:, at], held_ref.at[:, at], sem.at[k, 0]))
        for i, ref in enumerate(tokens):
            rows = ref.shape[0]
            copies.append(
                pltpu.make_async_copy(
                    ref.at[:, at], x_ref.at[pl.ds(i * rows, rows), at], sem.at[k, i + 1]
                )
            )
        parts.append(copies)
    return parts


def project_rows(parts, x_ref, held_ref, out_ref):
    depth = D // PARTS
    totals = [None] * 3
    for k, copies in enumerate(parts):
        for copy in copies:
            copy.wait()
        at = slice(k * depth, (k + 1) * depth)
        x = x_ref[:, at]
        for j in range(3):
            term = jnp.dot(x, held_ref[j, at], preferred_element_type=jnp.float32)
            totals[j] = term if totals[j] is None else totals[j] + term
    for j in range(3):
        for h in range(2):
            values = totals[j][:, h * HEAD : (h + 1) * HEAD]
            if j < 2:
                values = rms_scale(values)
            out_ref[j, :, h * HEAD : (h + 1) * HEAD] = values.astype(jnp.bfloat16)


def project_scratch(count, rows, ready):
    scratch = [pltpu.VMEM((rows, D), jnp.bfloat16), pltpu.SemaphoreType.DMA((PARTS, count + 1))]
    return scratch if ready else [*scratch, pltpu.VMEM((3, D, WIDTH), jnp.bfloat16)]


def project_body(count, *refs):
    tokens, (w_ref, out_ref, x_ref, sem, held_ref) = refs[:count], refs[count:]
    parts = project_copies(tokens, w_ref, x_ref, held_ref, sem)
    for copies in parts:
        for copy in copies:
            copy.start()
    project_rows(parts, x_ref, held_ref, out_ref)


def project(tokens, weights):
    count = len(tokens)
    rows = count * tokens[0].shape[0]
    return pl.pallas_call(
        lambda *refs: project_body(count, *refs),
        in_specs=[HBM] * (count + 1),
        out_specs=VMEM,
        scratch_shapes=project_scratch(count, rows, False),
        out_shape=jax.ShapeDtypeStruct((3, rows, WIDTH), jnp.bfloat16),
        compiler_params=pltpu.CompilerParams(vmem_limit_bytes=56 * MIB),
        cost_estimate=pl.CostEstimate(
            flops=2 * rows * D * 768, bytes_accessed=rows * D * 2, transcendentals=0
        ),
        name="project",
    )(*tokens, weights)


def finish_body(group, videos, ready, plan_ref, *refs):
    n = len(videos)
    steps, tokens, (w_ref, cache_ref) = refs[:3], refs[3:5], refs[5:7]
    scratch, held_ref = refs[-10:], w_ref
    if not ready:
        scratch, held_ref = refs[-11:-1], refs[-1]
    out_ref, old_ref, rows_ref, last_ref, step_ref, in_sem, out_sem, step_sem, x_ref, sem = scratch
    size = last_ref.shape[1]
    y, z, core = plan_ref[24], plan_ref[25], plan_ref[26]

    def fetch(i, g):
        place = plan_ref[videos[i]]
        return pltpu.make_async_copy(cache_ref.at[place, g], old_ref.at[i, g], in_sem.at[i, g])

    def store(i):
        return pltpu.make_async_copy(rows_ref.at[i], out_ref.at[videos[i]], out_sem.at[i])

    parts = project_copies(tokens, w_ref, x_ref, held_ref, sem)
    for copies in parts:
        for copy in copies:
            copy.start()
    for i in range(n):
        for g in range(MAXC):

            @pl.when(g < plan_ref[8 + videos[i]])
            def _():
                fetch(i, g).start()

    fetched = [
        pltpu.make_async_copy(
            step.at[:, pl.ds(group * size, size)], step_ref.at[k], step_sem.at[k]
        )
        for k, step in enumerate(steps)
    ]
    for copy in fetched:
        copy.start()

    project_rows(parts, x_ref, held_ref, last_ref)
    for copy in fetched:
        copy.wait()

    def current(i, j, lanes):
        half, place = i // (n // 2), i % (n // 2)
        pieces = []
        for step in (*(step_ref.at[k] for k in range(3)), last_ref):
            for block in range(4):
                at = (half * 4 * (n // 2) + block * (n // 2) + place) * ROWS
                pieces.append(step[j, at : at + ROWS, lanes])
        return jnp.concatenate(pieces, axis=0)

    def head(i, live, lanes):
        keys, values = [current(i, 1, lanes)], [current(i, 2, lanes)]
        for g in range(live):
            old = rms_scale(old_ref[i, g, 0, :, lanes].astype(jnp.float32))
            keys.append(old.astype(jnp.bfloat16))
            values.append(old_ref[i, g, 1, :, lanes])
        keys, values = jnp.concatenate(keys, axis=0), jnp.concatenate(values, axis=0)
        logits = lax.dot_general(
            current(i, 0, lanes), keys, (((1,), (1,)), ((), ())), preferred_element_type=jnp.float32
        )
        weights = jnp.exp2(logits * SCALE).astype(jnp.bfloat16)
        wide = jnp.concatenate([values, jnp.ones_like(values)], axis=1)
        both = jnp.dot(weights, wide, preferred_element_type=jnp.float32)
        return both[:, :HEAD] / both[:, HEAD:]

    for i in range(n):
        for live in range(1, MAXC + 1):

            @pl.when(plan_ref[8 + videos[i]] == live)
            def _():
                for g in range(live):
                    fetch(i, g).wait()
                out = [head(i, live, slice(h * HEAD, (h + 1) * HEAD)) for h in range(2)]
                out = jnp.concatenate(out, axis=1).astype(jnp.bfloat16)
                for step in range(4):
                    for block in range(4):
                        near, far = (0, -1, 1, 2)[block], -step if i < n // 2 else step
                        a = (y + jnp.where(core == 0, near, far)) & 3
                        b = (z + jnp.where(core == 0, far, near)) & 3
                        start = pl.multiple_of((a * 4 + b) * ROWS, ROWS)
                        at = (step * 4 + block) * ROWS
                        rows_ref[i, pl.ds(start, ROWS), :] = out[at : at + ROWS]

        store(i).start()
    for i in range(n):
        store(i).wait()


def finish(plan, group, videos, steps, tokens, weights, cache, earlier):
    ready = earlier is not None
    n = len(videos)
    rows = 2 * tokens[0].shape[0]
    given = [plan, *steps, *tokens, weights, cache]
    specs = [SMEM] + [HBM] * 5 + [VMEM if ready else HBM, HBM]
    aliases = {}
    if earlier is not None:
        aliases = {len(given): 0}
        given.append(earlier)
        specs.append(HBM)
    return pl.pallas_call(
        lambda *refs: finish_body(group, videos, ready, *refs),
        in_specs=specs,
        out_specs=HBM,
        scratch_shapes=[
            pltpu.VMEM((n,) + cache.shape[1:], jnp.bfloat16),
            pltpu.VMEM((n, GROUP, WIDTH), jnp.bfloat16),
            pltpu.VMEM((3, rows, WIDTH), jnp.bfloat16),
            pltpu.VMEM((3, 3, rows, WIDTH), jnp.bfloat16),
            pltpu.SemaphoreType.DMA((n, MAXC)),
            pltpu.SemaphoreType.DMA((n,)),
            pltpu.SemaphoreType.DMA((3,)),
            *project_scratch(2, rows, ready),
        ],
        out_shape=jax.ShapeDtypeStruct((8, GROUP, WIDTH), jnp.bfloat16),
        input_output_aliases=aliases,
        compiler_params=pltpu.CompilerParams(vmem_limit_bytes=(20 if ready else 50) * MIB),
        cost_estimate=pl.CostEstimate(
            flops=2 * rows * D * 768 + 4 * n * 2 * GROUP * 1280 * HEAD,
            bytes_accessed=n * MIB + rows * D * 2,
            transcendentals=n * 2 * GROUP * 1280,
        ),
        name="finish",
    )(*given)


def ring(phase, step):
    pairs = []
    for vid in range(8):
        for y in range(4):
            for z in range(4):
                if phase == vid % 2:
                    to = (y + step) % 4 * 4 + z
                else:
                    to = y * 4 + (z + step) % 4
                pairs.append((vid * 16 + y * 4 + z, vid * 16 + to))
    return pairs


def send(value, pairs):
    return lax.ppermute(value, ("vid", "fsdp"), pairs)


def after(value, *earlier):
    return lax.optimization_barrier((value, *earlier))[0]


def shards(latents, shift_mod, scale_mod, qkv_weight, kv_cache, holders, cached):
    weights = jnp.transpose(qkv_weight, (1, 0, 2))

    own = norm(latents, shift_mod, scale_mod, 2)
    below, above = send(own[0], ring(0, 1)), send(own[1], ring(0, -1))
    near = [
        (below, send(after(own[0], below), ring(0, -1))),
        (send(after(own[1], above), ring(0, 1)), above),
    ]
    ordered, plan = reorder(after(holders, below, above), cached, kv_cache)
    far = send(below, ring(0, 1)), send(above, ring(0, -1))
    far = after(far[0], far[1]), far[1]
    cache = lax.all_to_all(
        ordered, "vid", split_axis=0, concat_axis=0, tiled=True
    )

    groups = [[bundle([rows, *some, last])] for rows, some, last in zip(own, near, far)]
    sent, projected = [], []
    for step in range(4):
        for g, arrived in enumerate(groups):
            if step:
                one, two = arrived[-1]
                if len(sent) >= 2:
                    earlier = projected[: step - 1]
                    one = after(one, sent[-2][0], *earlier)
                    two = after(two, sent[-2][1], *earlier)
                sent.append((send(one, ring(1, 1)), send(two, ring(1, -1))))
                arrived.append(sent[-1])
        if step < 3:
            projected.append(project([*groups[0][-1], *groups[1][-1]], weights))
    out = None
    for g, videos in enumerate(((0, 1, 2, 3), (4, 5, 6, 7))):
        last = groups[g][-1]
        if out is not None:
            last = [after(rows, out) for rows in last]
        out = finish(plan, g, videos, projected, last, weights, cache, out)
    return out


def solution(mesh):
    return jax.shard_map(
        shards,
        mesh=mesh,
        in_specs=(
            P("vid", "fsdp", None),
            P("vid", None),
            P("vid", None),
            P(None, None, "fsdp"),
            P("vid", None, None, None, "fsdp"),
            P(),
            P(),
        ),
        out_specs=P("vid", None, "fsdp"),
        check_vma=False,
    )
```
